32 devices in a mesh: lat: 8 (over z, y), lon: 4 (over x, core).
Axes of the slice: x: 2, y: 2, z: 4, core: 2. Of those that a mesh axis runs over, the one named last changes fastest.
Arguments:
- fields: float32 [2, 96, 24, 512], P(None, 'lat', 'lon'), may hold values from -13 to 13, as said below
- grad_out: float32 [2, 96, 24, 512], P(None, 'lat', 'lon'), may hold values from -6 to 6
- region_ids: int32 [2, 96, 24], P(None, 'lat', 'lon'), may hold values from 0 to 2
- bias_index: int32 [144, 144], replicated, may hold values from 0 to 6335
- bias_table: float32 [6336, 16], replicated, may hold values from -4 to 4
- in_weight: float32 [512, 1536], replicated, may hold values from -5 to 5, as said below
- out_weight: float32 [512, 512], replicated, may hold values from -0.25 to 0.25
Outputs:
- grad_fields: float32 [2, 96, 24, 512], P(None, 'lat', 'lon')
- grad_in_weight: float32 [512, 1536], P('lon')
- grad_out_weight: float32 [512, 512], P('lon')
- grad_bias: float32 [6336, 16], P('lon')
The draws below stay inside these ranges and needn't reach their ends.
Inputs may be any that keep to these rules, and one draw needn't show every extreme that they name: `fields`: rows of the tokens have scales that differ widely. `in_weight`: Fan-in scaled; the query and key columns of each head carry a gain of their own.
All inputs are finite; a program needn't handle non-finite values.
Results may differ from the reference program's by a relative error of at most 0.0003.
Values sent between devices are 32-bit elements; how exact they have to be, the bound alone decides.
A program may use at most 128 MiB of HBM per device.

```python
import math
import jax
import jax.numpy as jnp
from jax import lax

WIDTH = 512
HEADS = 16
HEAD_DIM = 32
LEVELS = 2
WIN_LAT = 12
WIN_LON = 6
BIAS_ROWS = 6336
LAT_CELLS = 96
LON_CELLS = 24
WIN_TOKENS = 144


def draw_fields(key, part):
    key = jax.random.fold_in(key, 11)
    key_base, key_scale = jax.random.split(key, 2)
    full_shape = (LEVELS, LAT_CELLS, LON_CELLS, WIDTH)
    raw_values = jax.random.truncated_normal(key_base, -4.0, 4.0, full_shape, jnp.float32)
    scales = jnp.exp(jax.random.uniform(key_scale, full_shape[:3] + (1,), jnp.float32, math.log(0.3), math.log(3.0)))
    return raw_values * scales


def draw_in_weight(key, part):
    key = jax.random.fold_in(key, 12)
    key_base, key_heads = jax.random.split(key, 2)
    raw_weight = jax.random.truncated_normal(key_base, -4.0, 4.0, (WIDTH, 3 * WIDTH), jnp.float32) * WIDTH ** (-0.5)
    log_low, log_high = (math.log(0.5), math.log(2.0))
    head_gain = jnp.exp(jax.random.uniform(key_heads, (2, HEADS), jnp.float32, log_low, log_high))
    head_gain = jnp.concatenate([head_gain, jnp.ones((1, HEADS), jnp.float32)], axis=0)
    column_gain = jnp.repeat(head_gain, HEAD_DIM, axis=1).reshape(3 * WIDTH)
    return raw_weight * column_gain[None, :]


def place_ends(entries, own_key, smallest, high):
    longest = entries.shape.index(max(entries.shape))
    spots = []
    for shift in (0, 1):
        where = [jax.random.randint(jax.random.fold_in(own_key, axis), (), 0, length) for axis, length in enumerate(entries.shape)]
        where[longest] = (where[longest] + shift) % entries.shape[longest]
        spots.append(tuple(where))
    return entries.at[spots[0]].set(smallest).at[spots[1]].set(high)


def levels(rng, dims, cuts, low, high):
    gain, own = 1.0, jax.random.fold_in(rng, 6)
    for position, blocks in cuts:
        steps = jnp.exp(jax.random.uniform(jax.random.fold_in(own, position), (blocks,), jnp.float32, low / len(cuts), high / len(cuts)))
        gain = gain * jnp.repeat(steps, dims[position] // blocks).reshape([-1 if axis == position else 1 for axis in range(len(dims))])
    return gain


def centred(stream_key, shape, spread, limit, cuts=(), kind=jnp.bfloat16):
    gain = levels(stream_key, shape, cuts, -0.22, 0.18) if cuts else 1.0
    values = jax.random.normal(stream_key, shape, jnp.float32) * spread * gain
    return jnp.minimum(jnp.maximum(values, -limit), limit).astype(kind)


def setup_inputs(seed: int = 0) -> dict:
    arg_keys = jax.random.split(jax.random.key(seed), 8)
    return {
        "fields": draw_fields(jax.random.fold_in(arg_keys[7], 71), 0),
        "grad_out": centred(arg_keys[1], (LEVELS, LAT_CELLS, LON_CELLS, WIDTH), 1.0, 6.0, ((1, 8), (2, 4)), jnp.float32),
        "region_ids": place_ends(jax.random.randint(arg_keys[2], (LEVELS, LAT_CELLS, LON_CELLS), 0, 3), jax.random.fold_in(arg_keys[2], 1), 0, 2).astype(jnp.int32),
        "bias_index": place_ends(jax.random.randint(arg_keys[3], (WIN_TOKENS, WIN_TOKENS), 0, BIAS_ROWS), jax.random.fold_in(arg_keys[3], 1), 0, BIAS_ROWS - 1).astype(jnp.int32),
        "bias_table": centred(arg_keys[4], (BIAS_ROWS, HEADS), 1.0, 4.0, (), jnp.float32),
        "in_weight": draw_in_weight(jax.random.fold_in(arg_keys[7], 71), 0),
        "out_weight": centred(arg_keys[6], (WIDTH, WIDTH), WIDTH ** -0.5, 0.25, (), jnp.float32),
    }


def split_windows(array):
    level_count, row_count, col_count = array.shape[:3]
    trailing = array.shape[3:]
    blocked = array.reshape((level_count, row_count // WIN_LAT, WIN_LAT, col_count // WIN_LON, WIN_LON) + trailing)
    axis_order = (1, 3, 0, 2, 4) + tuple(range(5, 5 + len(trailing)))
    blocked = jnp.transpose(blocked, axis_order)
    return blocked.reshape((row_count // WIN_LAT * (col_count // WIN_LON), level_count * WIN_LAT * WIN_LON) + trailing)

def join_windows(windows, level_count, row_count, col_count):
    trailing = windows.shape[2:]
    blocked = windows.reshape((row_count // WIN_LAT, col_count // WIN_LON, level_count, WIN_LAT, WIN_LON) + trailing)
    axis_order = (2, 0, 3, 1, 4) + tuple(range(5, 5 + len(trailing)))
    blocked = jnp.transpose(blocked, axis_order)
    return blocked.reshape((level_count, row_count, col_count) + trailing)

def window_pass(inputs, cotangent, labels, owned, in_weight, out_weight, bias_full):
    highest = lax.Precision.HIGHEST
    average = lax.optimization_barrier(jnp.mean(inputs, axis=-1, keepdims=True))
    centered = inputs - average
    variance = lax.optimization_barrier(jnp.mean(centered * centered, axis=-1, keepdims=True))
    inv_std = lax.rsqrt(variance + 1e-05)
    normed = centered * inv_std
    projected = jnp.einsum('wtc,cf->wtf', normed, in_weight, precision=highest)
    win_count, tok_count = (inputs.shape[0], inputs.shape[1])
    heads_split = projected.reshape(win_count, tok_count, 3, HEADS, HEAD_DIM)
    queries = heads_split[:, :, 0]
    key_vecs = heads_split[:, :, 1]
    value_vecs = heads_split[:, :, 2]
    factor = HEAD_DIM ** (-0.5)
    scores = jnp.einsum('wqhd,wkhd->whqk', queries, key_vecs, precision=highest) * factor + bias_full[None]
    allowed = (labels[:, :, None] == labels[:, None, :]) & (labels[:, None, :] > 0.5)
    scores = jnp.where(allowed[:, None], scores, -1000000000.0)
    peak = lax.optimization_barrier(jnp.max(scores, axis=-1, keepdims=True))
    exponent = jnp.exp(scores - peak)
    probs = exponent / lax.optimization_barrier(jnp.sum(exponent, axis=-1, keepdims=True))
    attended = jnp.einsum('whqk,wkhd->wqhd', probs, value_vecs, precision=highest).reshape(win_count, tok_count, WIDTH)
    grad_attended = jnp.einsum('wte,ce->wtc', cotangent, out_weight, precision=highest)
    grad_out_part = jnp.einsum('wtc,wte->ce', attended * owned[..., None], cotangent, precision=highest)
    grad_heads = grad_attended.reshape(win_count, tok_count, HEADS, HEAD_DIM)
    grad_probs = jnp.einsum('wqhd,wkhd->whqk', grad_heads, value_vecs, precision=highest)
    grad_values = jnp.einsum('whqk,wqhd->wkhd', probs, grad_heads, precision=highest)
    grad_scores = probs * (grad_probs - lax.optimization_barrier(jnp.sum(grad_probs * probs, axis=-1, keepdims=True)))
    grad_queries = jnp.einsum('whqk,wkhd->wqhd', grad_scores, key_vecs, precision=highest) * factor
    grad_keys = jnp.einsum('whqk,wqhd->wkhd', grad_scores, queries, precision=highest) * factor
    score_sum = jnp.einsum('whqk,wq->hqk', grad_scores, owned, precision=highest)
    grad_projected = jnp.stack([grad_queries, grad_keys, grad_values], axis=2).reshape(win_count, tok_count, 3 * WIDTH)
    grad_in_part = jnp.einsum('wtc,wtf->cf', normed * owned[..., None], grad_projected, precision=highest)
    grad_normed = jnp.einsum('wtf,cf->wtc', grad_projected, in_weight, precision=highest)
    grad_inputs = inv_std * (grad_normed - lax.optimization_barrier(jnp.mean(grad_normed, axis=-1, keepdims=True)) - normed * lax.optimization_barrier(jnp.mean(grad_normed * normed, axis=-1, keepdims=True)))
    return (grad_inputs, grad_in_part, grad_out_part, score_sum)

def reference(fields, grad_out, region_ids, bias_index, bias_table, in_weight, out_weight):
    level_count, row_count, col_count, width = fields.shape
    half_rows = WIN_LAT // 2
    half_cols = WIN_LON // 2

    def prepare(array):
        pad_widths = ((0, 0), (half_rows, half_rows)) + ((0, 0),) * (array.ndim - 2)
        return jnp.roll(jnp.pad(array, pad_widths), -half_cols, axis=2)
    padded_in = prepare(fields)
    padded_grad = prepare(grad_out)
    padded_labels = prepare((region_ids + 1).astype(jnp.float32))
    bias_full = jnp.transpose(bias_table[bias_index], (2, 0, 1))
    band_count = (row_count + 2 * half_rows) // WIN_LAT

    def band_step(totals_so_far, band_number):
        first_row = band_number * WIN_LAT
        band_in = lax.dynamic_slice_in_dim(padded_in, first_row, WIN_LAT, 1)
        band_grad = lax.dynamic_slice_in_dim(padded_grad, first_row, WIN_LAT, 1)
        band_labels = lax.dynamic_slice_in_dim(padded_labels, first_row, WIN_LAT, 1)
        win_labels = split_windows(band_labels)
        owned = jnp.ones(win_labels.shape, jnp.float32)
        grad_win, part_in, part_out, part_scores = window_pass(split_windows(band_in), split_windows(band_grad), win_labels, owned, in_weight, out_weight, bias_full)
        new_totals = (totals_so_far[0] + part_in, totals_so_far[1] + part_out, totals_so_far[2] + part_scores)
        return (new_totals, join_windows(grad_win, level_count, WIN_LAT, col_count))
    zero_totals = (jnp.zeros((width, 3 * width), jnp.float32), jnp.zeros((width, width), jnp.float32), jnp.zeros((HEADS, WIN_TOKENS, WIN_TOKENS), jnp.float32))
    totals, banded = lax.scan(band_step, zero_totals, jnp.arange(band_count, dtype=jnp.int32))
    stacked = jnp.transpose(banded, (1, 0, 2, 3, 4)).reshape(level_count, band_count * WIN_LAT, col_count, width)
    grad_attn = jnp.roll(stacked[:, half_rows:half_rows + row_count], half_cols, axis=2)
    grad_fields = grad_out + grad_attn
    flat_scores = jnp.transpose(totals[2], (1, 2, 0)).reshape(-1, HEADS)
    grad_bias = jax.ops.segment_sum(flat_scores, bias_index.reshape(-1), num_segments=BIAS_ROWS)
    return (grad_fields, totals[0], totals[1], grad_bias)
```

```python
import jax
import jax.numpy as jnp
from jax import lax
from jax.sharding import PartitionSpec as P

WIDTH = 512
HEADS = 16
HEAD_DIM = 32
WIN_LAT = 12
WIN_LON = 6


def shifted(value, axis, steps):
    count = lax.axis_size(axis)
    pairs = [(source, (source + steps) % count) for source in range(count)]
    return lax.ppermute(value, axis, pairs)


def split_windows(array):
    level_count, row_count, col_count = array.shape[:3]
    trailing = array.shape[3:]
    blocked = array.reshape(
        (level_count, row_count // WIN_LAT, WIN_LAT, col_count // WIN_LON, WIN_LON) + trailing
    )
    axis_order = (1, 3, 0, 2, 4) + tuple(range(5, 5 + len(trailing)))
    blocked = jnp.transpose(blocked, axis_order)
    return blocked.reshape(
        (row_count // WIN_LAT * (col_count // WIN_LON), level_count * WIN_LAT * WIN_LON) + trailing
    )


def join_windows(windows, level_count, row_count, col_count):
    trailing = windows.shape[2:]
    blocked = windows.reshape(
        (row_count // WIN_LAT, col_count // WIN_LON, level_count, WIN_LAT, WIN_LON) + trailing
    )
    axis_order = (2, 0, 3, 1, 4) + tuple(range(5, 5 + len(trailing)))
    blocked = jnp.transpose(blocked, axis_order)
    return blocked.reshape((level_count, row_count, col_count) + trailing)


def window_pass(inputs, cotangent, labels, in_weight, out_weight, bias_full):
    highest = lax.Precision.HIGH
    average = jnp.mean(inputs, axis=-1, keepdims=True)
    centered = inputs - average
    variance = jnp.mean(centered * centered, axis=-1, keepdims=True)
    inv_std = lax.rsqrt(variance + 1e-05)
    normed = centered * inv_std
    projected = jnp.einsum("wtc,cf->wtf", normed, in_weight, precision=highest)
    win_count, tok_count = (inputs.shape[0], inputs.shape[1])
    heads_split = projected.reshape(win_count, tok_count, 3, HEADS, HEAD_DIM)
    queries = heads_split[:, :, 0]
    key_vecs = heads_split[:, :, 1]
    value_vecs = heads_split[:, :, 2]
    factor = HEAD_DIM ** (-0.5)
    scores = (
        jnp.einsum("wqhd,wkhd->whqk", queries, key_vecs, precision=highest) * factor
        + bias_full[None]
    )
    allowed = (labels[:, :, None] == labels[:, None, :]) & (labels[:, None, :] > 0.5)
    scores = jnp.where(allowed[:, None], scores, -1000000000.0)
    peak = jnp.max(scores, axis=-1, keepdims=True)
    exponent = jnp.exp(scores - peak)
    probs = exponent / jnp.sum(exponent, axis=-1, keepdims=True)
    attended = jnp.einsum("whqk,wkhd->wqhd", probs, value_vecs, precision=highest).reshape(
        win_count, tok_count, WIDTH
    )
    grad_attended = jnp.einsum("wte,ce->wtc", cotangent, out_weight, precision=highest)
    grad_out_part = jnp.einsum(
        "wtc,wte->ce", attended, cotangent, precision=highest
    )
    grad_heads = grad_attended.reshape(win_count, tok_count, HEADS, HEAD_DIM)
    grad_probs = jnp.einsum("wqhd,wkhd->whqk", grad_heads, value_vecs, precision=highest)
    grad_values = jnp.einsum("whqk,wqhd->wkhd", probs, grad_heads, precision=highest)
    grad_scores = probs * (grad_probs - jnp.sum(grad_probs * probs, axis=-1, keepdims=True))
    grad_queries = jnp.einsum("whqk,wkhd->wqhd", grad_scores, key_vecs, precision=highest) * factor
    grad_keys = jnp.einsum("whqk,wqhd->wkhd", grad_scores, queries, precision=highest) * factor
    score_sum = jnp.sum(grad_scores, axis=0)
    grad_projected = jnp.stack([grad_queries, grad_keys, grad_values], axis=2).reshape(
        win_count, tok_count, 3 * WIDTH
    )
    grad_in_part = jnp.einsum(
        "wtc,wtf->cf", normed, grad_projected, precision=highest
    )
    grad_normed = jnp.einsum("wtf,cf->wtc", grad_projected, in_weight, precision=highest)
    grad_inputs = inv_std * (
        grad_normed
        - jnp.mean(grad_normed, axis=-1, keepdims=True)
        - normed * jnp.mean(grad_normed * normed, axis=-1, keepdims=True)
    )
    return (grad_inputs, grad_in_part, grad_out_part, score_sum)


def rounded(value):
    return lax.reduce_precision(value, exponent_bits=8, mantissa_bits=7)


def three_terms(value, axis):
    first = rounded(value)
    second = rounded(value - first)
    third = rounded(value - first - second)
    return jnp.concatenate([first, second, third], axis=axis).astype(jnp.bfloat16)


def body(fields, grad_out, region_ids, bias_index, bias_table, in_weight, out_weight):
    level_count, row_count, col_count, width = fields.shape
    half_rows = WIN_LAT // 2
    half_cols = WIN_LON // 2
    token_count = bias_index.shape[0]
    table_rows, head_count = bias_table.shape
    lon_count = lax.axis_size("lon")
    device_count = lon_count * lax.axis_size("lat")
    device = lax.axis_index("lat") * lon_count + lax.axis_index("lon")
    pair_count = token_count * token_count // device_count
    own_index = lax.dynamic_slice_in_dim(
        bias_index.reshape(-1), device * pair_count, pair_count, 0
    )
    one_hot = (
        own_index[:, None] == jnp.arange(table_rows, dtype=jnp.int32)[None, :]
    ).astype(jnp.bfloat16)
    found = lax.dot_general(
        three_terms(bias_table, 1), one_hot, (((0,), (1,)), ((), ())),
        preferred_element_type=jnp.float32,
    )
    found = found[:head_count] + found[head_count : 2 * head_count] + found[2 * head_count :]
    gathered = lax.all_gather(found, ("lat", "lon"), axis=0)
    bias_full = jnp.transpose(gathered, (1, 0, 2)).reshape(head_count, token_count, token_count)

    labels = (region_ids + 1).astype(jnp.float32)
    label_lanes = jnp.broadcast_to(labels[..., None], labels.shape + (128,))
    block = jnp.concatenate([fields, grad_out, label_lanes], axis=3)
    block = jnp.concatenate(
        [block[:, :, half_cols:], shifted(block[:, :, :half_cols], "lon", -1)], axis=2
    )
    block = jnp.concatenate(
        [shifted(block[:, row_count - half_rows :], "lat", 1), block[:, : row_count - half_rows]],
        axis=1,
    )
    frame_in = block[..., :width]
    frame_grad = block[..., width : 2 * width]
    wrapped = (lax.axis_index("lat") == 0) & (jnp.arange(row_count) < half_rows)
    frame_labels = block[..., 2 * width] + jnp.where(wrapped, 3.0, 0.0)[None, :, None]
    grad_win, grad_in_part, grad_out_part, score_sum = window_pass(
        split_windows(frame_in),
        split_windows(frame_grad),
        split_windows(frame_labels),
        in_weight,
        out_weight,
        bias_full,
    )
    own_scores = lax.psum_scatter(
        jnp.transpose(score_sum.reshape(head_count, device_count, pair_count), (1, 0, 2)),
        ("lat", "lon"), scatter_dimension=0, tiled=True,
    )[0]
    found = jnp.dot(three_terms(own_scores, 0), one_hot, preferred_element_type=jnp.float32)
    found = found[:head_count] + found[head_count : 2 * head_count] + found[2 * head_count :]
    grad_bias = lax.psum(
        lax.psum_scatter(jnp.transpose(found), "lon", scatter_dimension=0, tiled=True), "lat"
    )
    weights_part = jnp.concatenate([grad_in_part, grad_out_part], axis=1)
    weights = lax.psum(
        lax.psum_scatter(weights_part, "lon", scatter_dimension=0, tiled=True), "lat"
    )
    grad_frame = join_windows(grad_win, level_count, row_count, col_count)
    grad_frame = jnp.concatenate(
        [grad_frame[:, half_rows:], shifted(grad_frame[:, :half_rows], "lat", -1)], axis=1
    )
    grad_frame = jnp.concatenate(
        [
            shifted(grad_frame[:, :, col_count - half_cols :], "lon", 1),
            grad_frame[:, :, : col_count - half_cols],
        ],
        axis=2,
    )
    return (grad_out + grad_frame, weights[:, : 3 * width], weights[:, 3 * width :], grad_bias)


def solution(mesh):
    in_specs = (
        P(None, "lat", "lon", None),
        P(None, "lat", "lon", None),
        P(None, "lat", "lon"),
        P(),
        P(),
        P(),
        P(),
    )
    out_specs = (P(None, "lat", "lon", None), P("lon", None), P("lon", None), P("lon", None))
    return jax.shard_map(body, mesh=mesh, in_specs=in_specs, out_specs=out_specs, check_vma=False)
```

```python
import jax
import jax.numpy as jnp
from jax import lax
from jax.sharding import PartitionSpec as P

WIDTH = 512
HEADS = 16
HEAD_DIM = 32
WIN_LAT = 12
WIN_LON = 6


def shifted(value, axis, steps):
    count = lax.axis_size(axis)
    pairs = [(source, (source + steps) % count) for source in range(count)]
    return lax.ppermute(value, axis, pairs)


def bit_count(axis):
    count = lax.axis_size(axis)
    assert count & (count - 1) == 0
    return count.bit_length() - 1


def swapped(value, axis, bit):
    count = lax.axis_size(axis)
    return lax.ppermute(value, axis, [(i, i ^ (1 << bit)) for i in range(count)])


def halved_sum(value, axis):
    index = lax.axis_index(axis)
    for bit in range(bit_count(axis)):
        value = value.reshape((value.shape[0] // 2, 2) + value.shape[1:])
        side = (index >> bit) & 1
        kept = lax.dynamic_index_in_dim(value, side, 1, keepdims=False)
        given = lax.dynamic_index_in_dim(value, 1 - side, 1, keepdims=False)
        value = kept + swapped(given, axis, bit)
    return value


def doubled(value, axis):
    index = lax.axis_index(axis)
    for bit in reversed(range(bit_count(axis))):
        other = swapped(value, axis, bit)
        upper = ((index >> bit) & 1) == 1
        low = jnp.where(upper, other, value)
        high = jnp.where(upper, value, other)
        value = jnp.stack([low, high], axis=1)
        value = value.reshape((value.shape[0] * 2,) + value.shape[2:])
    return value


def swapped_sum(value, axis):
    for bit in range(bit_count(axis)):
        value = value + swapped(value, axis, bit)
    return value


def split_windows(array):
    level_count, row_count, col_count = array.shape[:3]
    trailing = array.shape[3:]
    blocked = array.reshape(
        (level_count, row_count // WIN_LAT, WIN_LAT, col_count // WIN_LON, WIN_LON) + trailing
    )
    axis_order = (1, 3, 0, 2, 4) + tuple(range(5, 5 + len(trailing)))
    blocked = jnp.transpose(blocked, axis_order)
    return blocked.reshape(
        (row_count // WIN_LAT * (col_count // WIN_LON), level_count * WIN_LAT * WIN_LON) + trailing
    )


def join_windows(windows, level_count, row_count, col_count):
    trailing = windows.shape[2:]
    blocked = windows.reshape(
        (row_count // WIN_LAT, col_count // WIN_LON, level_count, WIN_LAT, WIN_LON) + trailing
    )
    axis_order = (2, 0, 3, 1, 4) + tuple(range(5, 5 + len(trailing)))
    blocked = jnp.transpose(blocked, axis_order)
    return blocked.reshape((level_count, row_count, col_count) + trailing)


def window_pass(inputs, cotangent, labels, in_weight, out_weight, bias_full):
    highest = lax.Precision.HIGH
    average = jnp.mean(inputs, axis=-1, keepdims=True)
    centered = inputs - average
    variance = jnp.mean(centered * centered, axis=-1, keepdims=True)
    inv_std = lax.rsqrt(variance + 1e-05)
    normed = centered * inv_std
    projected = jnp.einsum("wtc,cf->wtf", normed, in_weight, precision=highest)
    win_count, tok_count = (inputs.shape[0], inputs.shape[1])
    heads_split = projected.reshape(win_count, tok_count, 3, HEADS, HEAD_DIM)
    queries = heads_split[:, :, 0]
    key_vecs = heads_split[:, :, 1]
    value_vecs = heads_split[:, :, 2]
    factor = HEAD_DIM ** (-0.5)
    scores = (
        jnp.einsum("wqhd,wkhd->whqk", queries, key_vecs, precision=highest) * factor
        + bias_full[None]
    )
    allowed = (labels[:, :, None] == labels[:, None, :]) & (labels[:, None, :] > 0.5)
    scores = jnp.where(allowed[:, None], scores, -1000000000.0)
    peak = jnp.max(scores, axis=-1, keepdims=True)
    exponent = jnp.exp(scores - peak)
    probs = exponent / jnp.sum(exponent, axis=-1, keepdims=True)
    attended = jnp.einsum("whqk,wkhd->wqhd", probs, value_vecs, precision=highest).reshape(
        win_count, tok_count, WIDTH
    )
    grad_attended = jnp.einsum("wte,ce->wtc", cotangent, out_weight, precision=highest)
    grad_out_part = jnp.einsum(
        "wtc,wte->ce", attended, cotangent, precision=highest
    )
    grad_heads = grad_attended.reshape(win_count, tok_count, HEADS, HEAD_DIM)
    grad_probs = jnp.einsum("wqhd,wkhd->whqk", grad_heads, value_vecs, precision=highest)
    grad_values = jnp.einsum("whqk,wqhd->wkhd", probs, grad_heads, precision=highest)
    grad_scores = probs * (grad_probs - jnp.sum(grad_probs * probs, axis=-1, keepdims=True))
    grad_queries = jnp.einsum("whqk,wkhd->wqhd", grad_scores, key_vecs, precision=highest) * factor
    grad_keys = jnp.einsum("whqk,wqhd->wkhd", grad_scores, queries, precision=highest) * factor
    score_sum = jnp.sum(grad_scores, axis=0)
    grad_projected = jnp.stack([grad_queries, grad_keys, grad_values], axis=2).reshape(
        win_count, tok_count, 3 * WIDTH
    )
    grad_in_part = jnp.einsum(
        "wtc,wtf->cf", normed, grad_projected, precision=highest
    )
    grad_normed = jnp.einsum("wtf,cf->wtc", grad_projected, in_weight, precision=highest)
    grad_inputs = inv_std * (
        grad_normed
        - jnp.mean(grad_normed, axis=-1, keepdims=True)
        - normed * jnp.mean(grad_normed * normed, axis=-1, keepdims=True)
    )
    return (grad_inputs, grad_in_part, grad_out_part, score_sum)


def rounded(value):
    return lax.reduce_precision(value, exponent_bits=8, mantissa_bits=7)


def three_terms(value, axis):
    first = rounded(value)
    second = rounded(value - first)
    third = rounded(value - first - second)
    return jnp.concatenate([first, second, third], axis=axis).astype(jnp.bfloat16)


def body(fields, grad_out, region_ids, bias_index, bias_table, in_weight, out_weight):
    level_count, row_count, col_count, width = fields.shape
    half_rows = WIN_LAT // 2
    half_cols = WIN_LON // 2
    token_count = bias_index.shape[0]
    table_rows, head_count = bias_table.shape
    lon_count = lax.axis_size("lon")
    lat_count = lax.axis_size("lat")
    device_count = lon_count * lat_count
    device = lax.axis_index("lon") * lat_count + lax.axis_index("lat")
    pair_count = token_count * token_count // device_count
    own_index = lax.dynamic_slice_in_dim(
        bias_index.reshape(-1), device * pair_count, pair_count, 0
    )
    one_hot = (
        own_index[:, None] == jnp.arange(table_rows, dtype=jnp.int32)[None, :]
    ).astype(jnp.bfloat16)
    found = lax.dot_general(
        three_terms(bias_table, 1), one_hot, (((0,), (1,)), ((), ())),
        preferred_element_type=jnp.float32,
    )
    found = found[:head_count] + found[head_count : 2 * head_count] + found[2 * head_count :]
    gathered = doubled(doubled(found[None], "lat")[None], "lon").reshape(
        device_count, head_count, pair_count
    )
    bias_full = jnp.transpose(gathered, (1, 0, 2)).reshape(head_count, token_count, token_count)

    labels = (region_ids + 1).astype(jnp.float32)
    label_lanes = jnp.broadcast_to(labels[..., None], labels.shape + (128,))
    block = jnp.concatenate([fields, grad_out, label_lanes], axis=3)
    block = jnp.concatenate(
        [block[:, :, half_cols:], shifted(block[:, :, :half_cols], "lon", -1)], axis=2
    )
    block = jnp.concatenate(
        [shifted(block[:, row_count - half_rows :], "lat", 1), block[:, : row_count - half_rows]],
        axis=1,
    )
    frame_in = block[..., :width]
    frame_grad = block[..., width : 2 * width]
    wrapped = (lax.axis_index("lat") == 0) & (jnp.arange(row_count) < half_rows)
    frame_labels = block[..., 2 * width] + jnp.where(wrapped, 3.0, 0.0)[None, :, None]
    grad_win, grad_in_part, grad_out_part, score_sum = window_pass(
        split_windows(frame_in),
        split_windows(frame_grad),
        split_windows(frame_labels),
        in_weight,
        out_weight,
        bias_full,
    )
    score_parts = jnp.transpose(
        score_sum.reshape(head_count, device_count, pair_count), (1, 0, 2)
    ).reshape(lon_count, lat_count, head_count, pair_count)
    own_scores = halved_sum(halved_sum(score_parts, "lon")[0], "lat")[0]
    found = jnp.dot(three_terms(own_scores, 0), one_hot, preferred_element_type=jnp.float32)
    found = found[:head_count] + found[head_count : 2 * head_count] + found[2 * head_count :]
    found = jnp.transpose(
        found.reshape(head_count, lon_count, table_rows // lon_count), (1, 0, 2)
    )
    grad_bias = jnp.transpose(swapped_sum(halved_sum(found, "lon")[0], "lat"))
    weights_part = jnp.concatenate([grad_in_part, grad_out_part], axis=1)
    own_rows = width // lon_count
    weights_part = weights_part.reshape(lon_count, own_rows, 4 * width)
    weights = halved_sum(weights_part, "lon").reshape(lat_count, own_rows // lat_count, 4 * width)
    weights = doubled(halved_sum(weights, "lat"), "lat").reshape(own_rows, 4 * width)
    grad_frame = join_windows(grad_win, level_count, row_count, col_count)
    grad_frame = jnp.concatenate(
        [grad_frame[:, half_rows:], shifted(grad_frame[:, :half_rows], "lat", -1)], axis=1
    )
    grad_frame = jnp.concatenate(
        [
            shifted(grad_frame[:, :, col_count - half_cols :], "lon", 1),
            grad_frame[:, :, : col_count - half_cols],
        ],
        axis=2,
    )
    return (grad_out + grad_frame, weights[:, : 3 * width], weights[:, 3 * width :], grad_bias)


def solution(mesh):
    in_specs = (
        P(None, "lat", "lon", None),
        P(None, "lat", "lon", None),
        P(None, "lat", "lon"),
        P(),
        P(),
        P(),
        P(),
    )
    out_specs = (P(None, "lat", "lon", None), P("lon", None), P("lon", None), P("lon", None))
    return jax.shard_map(body, mesh=mesh, in_specs=in_specs, out_specs=out_specs, check_vma=False)
```

```python
import jax
import jax.numpy as jnp
from jax import lax
from jax.sharding import PartitionSpec as P

WIDTH = 512
HEADS = 16
HEAD_DIM = 32
WIN_LAT = 12
WIN_LON = 6


def shifted(value, axis, steps):
    count = lax.axis_size(axis)
    pairs = [(source, (source + steps) % count) for source in range(count)]
    return lax.ppermute(value, axis, pairs)


def bit_count(axis):
    count = lax.axis_size(axis)
    assert count & (count - 1) == 0
    return count.bit_length() - 1


def swapped(value, axis, bit):
    count = lax.axis_size(axis)
    return lax.ppermute(value, axis, [(i, i ^ (1 << bit)) for i in range(count)])


def halved_sum(value, axis):
    index = lax.axis_index(axis)
    for bit in range(bit_count(axis)):
        value = value.reshape((value.shape[0] // 2, 2) + value.shape[1:])
        side = (index >> bit) & 1
        kept = lax.dynamic_index_in_dim(value, side, 1, keepdims=False)
        given = lax.dynamic_index_in_dim(value, 1 - side, 1, keepdims=False)
        value = kept + swapped(given, axis, bit)
    return value


def doubled(value, axis):
    index = lax.axis_index(axis)
    for bit in reversed(range(bit_count(axis))):
        other = swapped(value, axis, bit)
        upper = ((index >> bit) & 1) == 1
        low = jnp.where(upper, other, value)
        high = jnp.where(upper, value, other)
        value = jnp.stack([low, high], axis=1)
        value = value.reshape((value.shape[0] * 2,) + value.shape[2:])
    return value


def swapped_sum(value, axis):
    for bit in range(bit_count(axis)):
        value = value + swapped(value, axis, bit)
    return value


def split_windows(array):
    level_count, row_count, col_count = array.shape[:3]
    trailing = array.shape[3:]
    blocked = array.reshape(
        (level_count, row_count // WIN_LAT, WIN_LAT, col_count // WIN_LON, WIN_LON) + trailing
    )
    axis_order = (1, 3, 0, 2, 4) + tuple(range(5, 5 + len(trailing)))
    blocked = jnp.transpose(blocked, axis_order)
    return blocked.reshape(
        (row_count // WIN_LAT * (col_count // WIN_LON), level_count * WIN_LAT * WIN_LON) + trailing
    )


def join_windows(windows, level_count, row_count, col_count):
    trailing = windows.shape[2:]
    blocked = windows.reshape(
        (row_count // WIN_LAT, col_count // WIN_LON, level_count, WIN_LAT, WIN_LON) + trailing
    )
    axis_order = (2, 0, 3, 1, 4) + tuple(range(5, 5 + len(trailing)))
    blocked = jnp.transpose(blocked, axis_order)
    return blocked.reshape((level_count, row_count, col_count) + trailing)


def window_pass(inputs, cotangent, labels, in_weight, out_weight, bias_full):
    highest = lax.Precision.HIGH
    average = jnp.mean(inputs, axis=-1, keepdims=True)
    centered = inputs - average
    variance = jnp.mean(centered * centered, axis=-1, keepdims=True)
    inv_std = lax.rsqrt(variance + 1e-05)
    normed = centered * inv_std
    projected = jnp.einsum("wtc,cf->wtf", normed, in_weight, precision=highest)
    win_count, tok_count = (inputs.shape[0], inputs.shape[1])
    heads_split = projected.reshape(win_count, tok_count, 3, HEADS, HEAD_DIM)
    queries = heads_split[:, :, 0]
    key_vecs = heads_split[:, :, 1]
    value_vecs = heads_split[:, :, 2]
    factor = HEAD_DIM ** (-0.5)
    scores = (
        jnp.einsum("wqhd,wkhd->whqk", queries, key_vecs, precision=highest) * factor
        + bias_full[None]
    )
    allowed = (labels[:, :, None] == labels[:, None, :]) & (labels[:, None, :] > 0.5)
    scores = jnp.where(allowed[:, None], scores, -1000000000.0)
    peak = jnp.max(scores, axis=-1, keepdims=True)
    exponent = jnp.exp(scores - peak)
    probs = exponent / jnp.sum(exponent, axis=-1, keepdims=True)
    attended = jnp.einsum("whqk,wkhd->wqhd", probs, value_vecs, precision=highest).reshape(
        win_count, tok_count, WIDTH
    )
    grad_attended = jnp.einsum("wte,ce->wtc", cotangent, out_weight, precision=highest)
    grad_out_part = jnp.einsum(
        "wtc,wte->ce", attended, cotangent, precision=highest
    )
    grad_heads = grad_attended.reshape(win_count, tok_count, HEADS, HEAD_DIM)
    grad_probs = jnp.einsum("wqhd,wkhd->whqk", grad_heads, value_vecs, precision=highest)
    grad_values = jnp.einsum("whqk,wqhd->wkhd", probs, grad_heads, precision=highest)
    grad_scores = probs * (grad_probs - jnp.sum(grad_probs * probs, axis=-1, keepdims=True))
    grad_queries = jnp.einsum("whqk,wkhd->wqhd", grad_scores, key_vecs, precision=highest) * factor
    grad_keys = jnp.einsum("whqk,wqhd->wkhd", grad_scores, queries, precision=highest) * factor
    score_sum = jnp.sum(grad_scores, axis=0)
    grad_projected = jnp.stack([grad_queries, grad_keys, grad_values], axis=2).reshape(
        win_count, tok_count, 3 * WIDTH
    )
    grad_in_part = jnp.einsum(
        "wtc,wtf->cf", normed, grad_projected, precision=highest
    )
    grad_normed = jnp.einsum("wtf,cf->wtc", grad_projected, in_weight, precision=highest)
    grad_inputs = inv_std * (
        grad_normed
        - jnp.mean(grad_normed, axis=-1, keepdims=True)
        - normed * jnp.mean(grad_normed * normed, axis=-1, keepdims=True)
    )
    return (grad_inputs, grad_in_part, grad_out_part, score_sum)


def rounded(value):
    return lax.reduce_precision(value, exponent_bits=8, mantissa_bits=7)


def three_terms(value, axis):
    first = rounded(value)
    second = rounded(value - first)
    third = rounded(value - first - second)
    return jnp.concatenate([first, second, third], axis=axis).astype(jnp.bfloat16)


def body(fields, grad_out, region_ids, bias_index, bias_table, in_weight, out_weight):
    level_count, row_count, col_count, width = fields.shape
    half_rows = WIN_LAT // 2
    half_cols = WIN_LON // 2
    token_count = bias_index.shape[0]
    table_rows, head_count = bias_table.shape
    lon_count = lax.axis_size("lon")
    lat_count = lax.axis_size("lat")
    device_count = lon_count * lat_count
    device = lax.axis_index("lon") * lat_count + lax.axis_index("lat")
    pair_count = token_count * token_count // device_count
    own_index = lax.dynamic_slice_in_dim(
        bias_index.reshape(-1), device * pair_count, pair_count, 0
    )
    one_hot = (
        own_index[:, None] == jnp.arange(table_rows, dtype=jnp.int32)[None, :]
    ).astype(jnp.bfloat16)
    found = lax.dot_general(
        three_terms(bias_table, 1), one_hot, (((0,), (1,)), ((), ())),
        preferred_element_type=jnp.float32,
    )
    found = found[:head_count] + found[head_count : 2 * head_count] + found[2 * head_count :]
    labels = (region_ids + 1).astype(jnp.float32)
    label_lanes = jnp.broadcast_to(labels[..., None], labels.shape + (128,))
    block = jnp.concatenate([fields, grad_out, label_lanes], axis=3)
    block = jnp.concatenate(
        [block[:, :, half_cols:], shifted(block[:, :, :half_cols], "lon", -1)], axis=2
    )
    block = jnp.concatenate(
        [shifted(block[:, row_count - half_rows :], "lat", 1), block[:, : row_count - half_rows]],
        axis=1,
    )
    block, found = lax.optimization_barrier((block, found))
    gathered = doubled(doubled(found[None], "lat")[None], "lon").reshape(
        device_count, head_count, pair_count
    )
    bias_full = jnp.transpose(gathered, (1, 0, 2)).reshape(head_count, token_count, token_count)

    frame_in = block[..., :width]
    frame_grad = block[..., width : 2 * width]
    wrapped = (lax.axis_index("lat") == 0) & (jnp.arange(row_count) < half_rows)
    frame_labels = block[..., 2 * width] + jnp.where(wrapped, 3.0, 0.0)[None, :, None]
    grad_win, grad_in_part, grad_out_part, score_sum = window_pass(
        split_windows(frame_in),
        split_windows(frame_grad),
        split_windows(frame_labels),
        in_weight,
        out_weight,
        bias_full,
    )
    score_parts = jnp.transpose(
        score_sum.reshape(head_count, device_count, pair_count), (1, 0, 2)
    ).reshape(lon_count, lat_count, head_count, pair_count)
    own_scores = halved_sum(halved_sum(score_parts, "lon")[0], "lat")[0]
    found = jnp.dot(three_terms(own_scores, 0), one_hot, preferred_element_type=jnp.float32)
    found = found[:head_count] + found[head_count : 2 * head_count] + found[2 * head_count :]
    found = jnp.transpose(
        found.reshape(head_count, lon_count, table_rows // lon_count), (1, 0, 2)
    )
    grad_bias = jnp.transpose(swapped_sum(halved_sum(found, "lon")[0], "lat"))
    weights_part = jnp.concatenate([grad_in_part, grad_out_part], axis=1)
    own_rows = width // lon_count
    weights_part = weights_part.reshape(lon_count, own_rows, 4 * width)
    weights = halved_sum(weights_part, "lon").reshape(lat_count, own_rows // lat_count, 4 * width)
    weights = doubled(halved_sum(weights, "lat"), "lat").reshape(own_rows, 4 * width)
    grad_frame = join_windows(grad_win, level_count, row_count, col_count)
    grad_frame = jnp.concatenate(
        [grad_frame[:, half_rows:], shifted(grad_frame[:, :half_rows], "lat", -1)], axis=1
    )
    grad_frame = jnp.concatenate(
        [
            shifted(grad_frame[:, :, col_count - half_cols :], "lon", 1),
            grad_frame[:, :, : col_count - half_cols],
        ],
        axis=2,
    )
    return (grad_out + grad_frame, weights[:, : 3 * width], weights[:, 3 * width :], grad_bias)


def solution(mesh):
    in_specs = (
        P(None, "lat", "lon", None),
        P(None, "lat", "lon", None),
        P(None, "lat", "lon"),
        P(),
        P(),
        P(),
        P(),
    )
    out_specs = (P(None, "lat", "lon", None), P("lon", None), P("lon", None), P("lon", None))
    return jax.shard_map(body, mesh=mesh, in_specs=in_specs, out_specs=out_specs, check_vma=False)
```

```python
import jax
import jax.numpy as jnp
from jax import lax
from jax.sharding import PartitionSpec as P

WIDTH = 512
HEADS = 16
HEAD_DIM = 32
WIN_LAT = 12
WIN_LON = 6


def shifted(value, axis, steps):
    count = lax.axis_size(axis)
    pairs = [(source, (source + steps) % count) for source in range(count)]
    return lax.ppermute(value, axis, pairs)


def bit_count(axis):
    count = lax.axis_size(axis)
    assert count & (count - 1) == 0
    return count.bit_length() - 1


def swapped(value, axis, bit):
    count = lax.axis_size(axis)
    return lax.ppermute(value, axis, [(i, i ^ (1 << bit)) for i in range(count)])


def halved_sum(value, axis):
    index = lax.axis_index(axis)
    for bit in range(bit_count(axis)):
        value = value.reshape((value.shape[0] // 2, 2) + value.shape[1:])
        side = (index >> bit) & 1
        kept = lax.dynamic_index_in_dim(value, side, 1, keepdims=False)
        given = lax.dynamic_index_in_dim(value, 1 - side, 1, keepdims=False)
        value = kept + swapped(given, axis, bit)
    return value


def halved_steps(value, order):
    left = [(axis, bit) for axis in ("lon", "lat") for bit in reversed(range(bit_count(axis)))]
    value = value.reshape((2,) * len(left) + value.shape[2:])
    for axis, bit in order:
        dim = left.index((axis, bit))
        left.remove((axis, bit))
        side = (lax.axis_index(axis) >> bit) & 1
        kept = lax.dynamic_index_in_dim(value, side, dim, keepdims=False)
        given = lax.dynamic_index_in_dim(value, 1 - side, dim, keepdims=False)
        value = kept + swapped(given, axis, bit)
        yield value


def doubled(value, axis):
    index = lax.axis_index(axis)
    for bit in reversed(range(bit_count(axis))):
        other = swapped(value, axis, bit)
        upper = ((index >> bit) & 1) == 1
        low = jnp.where(upper, other, value)
        high = jnp.where(upper, value, other)
        value = jnp.stack([low, high], axis=1)
        value = value.reshape((value.shape[0] * 2,) + value.shape[2:])
    return value


def swapped_sum(value, axis):
    for bit in range(bit_count(axis)):
        value = value + swapped(value, axis, bit)
    return value


def split_windows(array):
    level_count, row_count, col_count = array.shape[:3]
    trailing = array.shape[3:]
    blocked = array.reshape(
        (level_count, row_count // WIN_LAT, WIN_LAT, col_count // WIN_LON, WIN_LON) + trailing
    )
    axis_order = (1, 3, 0, 2, 4) + tuple(range(5, 5 + len(trailing)))
    blocked = jnp.transpose(blocked, axis_order)
    return blocked.reshape(
        (row_count // WIN_LAT * (col_count // WIN_LON), level_count * WIN_LAT * WIN_LON) + trailing
    )


def join_windows(windows, level_count, row_count, col_count):
    trailing = windows.shape[2:]
    blocked = windows.reshape(
        (row_count // WIN_LAT, col_count // WIN_LON, level_count, WIN_LAT, WIN_LON) + trailing
    )
    axis_order = (2, 0, 3, 1, 4) + tuple(range(5, 5 + len(trailing)))
    blocked = jnp.transpose(blocked, axis_order)
    return blocked.reshape((level_count, row_count, col_count) + trailing)


def window_pass(inputs, cotangent, labels, in_weight, out_weight, bias_full):
    highest = lax.Precision.HIGH
    average = jnp.mean(inputs, axis=-1, keepdims=True)
    centered = inputs - average
    variance = jnp.mean(centered * centered, axis=-1, keepdims=True)
    inv_std = lax.rsqrt(variance + 1e-05)
    normed = centered * inv_std
    projected = jnp.einsum("wtc,cf->wtf", normed, in_weight, precision=highest)
    win_count, tok_count = (inputs.shape[0], inputs.shape[1])
    heads_split = projected.reshape(win_count, tok_count, 3, HEADS, HEAD_DIM)
    queries = heads_split[:, :, 0]
    key_vecs = heads_split[:, :, 1]
    value_vecs = heads_split[:, :, 2]
    factor = HEAD_DIM ** (-0.5)
    scores = (
        jnp.einsum("wqhd,wkhd->whqk", queries, key_vecs, precision=highest) * factor
        + bias_full[None]
    )
    allowed = (labels[:, :, None] == labels[:, None, :]) & (labels[:, None, :] > 0.5)
    scores = jnp.where(allowed[:, None], scores, -1000000000.0)
    peak = jnp.max(scores, axis=-1, keepdims=True)
    exponent = jnp.exp(scores - peak)
    probs = exponent / jnp.sum(exponent, axis=-1, keepdims=True)
    attended = jnp.einsum("whqk,wkhd->wqhd", probs, value_vecs, precision=highest).reshape(
        win_count, tok_count, WIDTH
    )
    grad_attended = jnp.einsum("wte,ce->wtc", cotangent, out_weight, precision=highest)
    grad_out_part = jnp.einsum(
        "wtc,wte->ce", attended, cotangent, precision=highest
    )
    grad_heads = grad_attended.reshape(win_count, tok_count, HEADS, HEAD_DIM)
    grad_probs = jnp.einsum("wqhd,wkhd->whqk", grad_heads, value_vecs, precision=highest)
    grad_values = jnp.einsum("whqk,wqhd->wkhd", probs, grad_heads, precision=highest)
    grad_scores = probs * (grad_probs - jnp.sum(grad_probs * probs, axis=-1, keepdims=True))
    grad_queries = jnp.einsum("whqk,wkhd->wqhd", grad_scores, key_vecs, precision=highest) * factor
    grad_keys = jnp.einsum("whqk,wqhd->wkhd", grad_scores, queries, precision=highest) * factor
    score_sum = jnp.sum(grad_scores, axis=0)
    grad_values = grad_values.reshape(win_count, tok_count, WIDTH)
    grad_in_values = jnp.einsum("wtc,wtf->cf", normed, grad_values, precision=highest)
    grad_pairs = jnp.stack([grad_queries, grad_keys], axis=2).reshape(
        win_count, tok_count, 2 * WIDTH
    )
    grad_in_pairs = jnp.einsum("wtc,wtf->cf", normed, grad_pairs, precision=highest)
    grad_projected = jnp.concatenate([grad_pairs, grad_values], axis=2)
    grad_normed = jnp.einsum("wtf,cf->wtc", grad_projected, in_weight, precision=highest)
    grad_inputs = inv_std * (
        grad_normed
        - jnp.mean(grad_normed, axis=-1, keepdims=True)
        - normed * jnp.mean(grad_normed * normed, axis=-1, keepdims=True)
    )
    return (grad_inputs, grad_in_pairs, grad_in_values, grad_out_part, score_sum)


def rounded(value):
    return lax.reduce_precision(value, exponent_bits=8, mantissa_bits=7)


def three_terms(value, axis):
    first = rounded(value)
    second = rounded(value - first)
    third = rounded(value - first - second)
    return jnp.concatenate([first, second, third], axis=axis).astype(jnp.bfloat16)


def body(fields, grad_out, region_ids, bias_index, bias_table, in_weight, out_weight):
    level_count, row_count, col_count, width = fields.shape
    half_rows = WIN_LAT // 2
    half_cols = WIN_LON // 2
    token_count = bias_index.shape[0]
    table_rows, head_count = bias_table.shape
    lon_count = lax.axis_size("lon")
    lat_count = lax.axis_size("lat")
    device_count = lon_count * lat_count
    device = lax.axis_index("lon") * lat_count + lax.axis_index("lat")
    pair_count = token_count * token_count // device_count
    own_index = lax.dynamic_slice_in_dim(
        bias_index.reshape(-1), device * pair_count, pair_count, 0
    )
    one_hot = (
        own_index[:, None] == jnp.arange(table_rows, dtype=jnp.int32)[None, :]
    ).astype(jnp.bfloat16)
    found = lax.dot_general(
        three_terms(bias_table, 1), one_hot, (((0,), (1,)), ((), ())),
        preferred_element_type=jnp.float32,
    )
    found = found[:head_count] + found[head_count : 2 * head_count] + found[2 * head_count :]
    labels = (region_ids + 1).astype(jnp.float32)
    label_lanes = jnp.broadcast_to(labels[..., None], labels.shape + (128,))
    block = jnp.concatenate([fields, grad_out, label_lanes], axis=3)
    block = jnp.concatenate(
        [block[:, :, half_cols:], shifted(block[:, :, :half_cols], "lon", -1)], axis=2
    )
    block = jnp.concatenate(
        [shifted(block[:, row_count - half_rows :], "lat", 1), block[:, : row_count - half_rows]],
        axis=1,
    )
    block, found = lax.optimization_barrier((block, found))
    gathered = doubled(doubled(found[None], "lat")[None], "lon").reshape(
        device_count, head_count, pair_count
    )
    bias_full = jnp.transpose(gathered, (1, 0, 2)).reshape(head_count, token_count, token_count)

    frame_in = block[..., :width]
    frame_grad = block[..., width : 2 * width]
    wrapped = (lax.axis_index("lat") == 0) & (jnp.arange(row_count) < half_rows)
    frame_labels = block[..., 2 * width] + jnp.where(wrapped, 3.0, 0.0)[None, :, None]
    grad_win, grad_in_pairs, grad_in_values, grad_out_part, score_sum = window_pass(
        split_windows(frame_in),
        split_windows(frame_grad),
        split_windows(frame_labels),
        in_weight,
        out_weight,
        bias_full,
    )
    own_rows = width // lon_count
    split = (lon_count, lat_count, own_rows // lat_count, 2 * width)
    lon_bits = [("lon", bit) for bit in range(bit_count("lon"))]
    lat_bits = [("lat", bit) for bit in range(bit_count("lat"))]
    late_part = jnp.concatenate([grad_in_values, grad_out_part], axis=1).reshape(split)
    late_steps = list(
        halved_steps(late_part, lon_bits[:1] + lat_bits[:1] + lon_bits[1:] + lat_bits[1:])
    )
    pair_steps = list(halved_steps(grad_in_pairs.reshape(split), lon_bits + lat_bits))
    late_weights = doubled(late_steps[-1][None], "lat").reshape(own_rows, 2 * width)
    pair_weights = doubled(pair_steps[-1][None], "lat").reshape(own_rows, 2 * width)
    score_parts = jnp.transpose(
        score_sum.reshape(head_count, device_count, pair_count), (1, 0, 2)
    ).reshape(lon_count, lat_count, head_count, pair_count)
    score_parts, _ = lax.optimization_barrier((score_parts, late_steps[0]))
    own_scores = halved_sum(halved_sum(score_parts, "lon")[0], "lat")[0]
    found = jnp.dot(three_terms(own_scores, 0), one_hot, preferred_element_type=jnp.float32)
    found = found[:head_count] + found[head_count : 2 * head_count] + found[2 * head_count :]
    found = jnp.transpose(
        found.reshape(head_count, lon_count, table_rows // lon_count), (1, 0, 2)
    )
    grad_bias = jnp.transpose(swapped_sum(halved_sum(found, "lon")[0], "lat"))
    grad_frame = join_windows(grad_win, level_count, row_count, col_count)
    grad_frame = jnp.concatenate(
        [grad_frame[:, half_rows:], shifted(grad_frame[:, :half_rows], "lat", -1)], axis=1
    )
    grad_frame = jnp.concatenate(
        [
            shifted(grad_frame[:, :, col_count - half_cols :], "lon", 1),
            grad_frame[:, :, : col_count - half_cols],
        ],
        axis=2,
    )
    grad_in_weight = jnp.concatenate([pair_weights, late_weights[:, :width]], axis=1)
    return (grad_out + grad_frame, grad_in_weight, late_weights[:, width:], grad_bias)


def solution(mesh):
    in_specs = (
        P(None, "lat", "lon", None),
        P(None, "lat", "lon", None),
        P(None, "lat", "lon"),
        P(),
        P(),
        P(),
        P(),
    )
    out_specs = (P(None, "lat", "lon", None), P("lon", None), P("lon", None), P("lon", None))
    return jax.shard_map(body, mesh=mesh, in_specs=in_specs, out_specs=out_specs, check_vma=False)
```

```python
import jax
import jax.numpy as jnp
from jax import lax
from jax.sharding import PartitionSpec as P

WIDTH = 512
HEADS = 16
HEAD_DIM = 32
WIN_LAT = 12
WIN_LON = 6


def shifted(value, axis, steps):
    count = lax.axis_size(axis)
    pairs = [(source, (source + steps) % count) for source in range(count)]
    return lax.ppermute(value, axis, pairs)


def bit_count(axis):
    count = lax.axis_size(axis)
    assert count & (count - 1) == 0
    return count.bit_length() - 1


def swapped(value, axis, bit):
    count = lax.axis_size(axis)
    return lax.ppermute(value, axis, [(i, i ^ (1 << bit)) for i in range(count)])


def halved_sum(value, axis):
    index = lax.axis_index(axis)
    for bit in range(bit_count(axis)):
        value = value.reshape((value.shape[0] // 2, 2) + value.shape[1:])
        side = (index >> bit) & 1
        kept = lax.dynamic_index_in_dim(value, side, 1, keepdims=False)
        given = lax.dynamic_index_in_dim(value, 1 - side, 1, keepdims=False)
        value = kept + swapped(given, axis, bit)
    return value


def halved_steps(value, order):
    left = [(axis, bit) for axis in ("lon", "lat") for bit in reversed(range(bit_count(axis)))]
    value = value.reshape((2,) * len(left) + value.shape[2:])
    for axis, bit in order:
        dim = left.index((axis, bit))
        left.remove((axis, bit))
        side = (lax.axis_index(axis) >> bit) & 1
        kept = lax.dynamic_index_in_dim(value, side, dim, keepdims=False)
        given = lax.dynamic_index_in_dim(value, 1 - side, dim, keepdims=False)
        value = kept + swapped(given, axis, bit)
        yield value


def doubled(value, axis):
    index = lax.axis_index(axis)
    for bit in reversed(range(bit_count(axis))):
        other = swapped(value, axis, bit)
        upper = ((index >> bit) & 1) == 1
        low = jnp.where(upper, other, value)
        high = jnp.where(upper, value, other)
        value = jnp.stack([low, high], axis=1)
        value = value.reshape((value.shape[0] * 2,) + value.shape[2:])
    return value


def swapped_sum(value, axis):
    for bit in range(bit_count(axis)):
        value = value + swapped(value, axis, bit)
    return value


def split_windows(array):
    level_count, row_count, col_count = array.shape[:3]
    trailing = array.shape[3:]
    blocked = array.reshape(
        (level_count, row_count // WIN_LAT, WIN_LAT, col_count // WIN_LON, WIN_LON) + trailing
    )
    axis_order = (1, 3, 0, 2, 4) + tuple(range(5, 5 + len(trailing)))
    blocked = jnp.transpose(blocked, axis_order)
    return blocked.reshape(
        (row_count // WIN_LAT * (col_count // WIN_LON), level_count * WIN_LAT * WIN_LON) + trailing
    )


def join_windows(windows, level_count, row_count, col_count):
    trailing = windows.shape[2:]
    blocked = windows.reshape(
        (row_count // WIN_LAT, col_count // WIN_LON, level_count, WIN_LAT, WIN_LON) + trailing
    )
    axis_order = (2, 0, 3, 1, 4) + tuple(range(5, 5 + len(trailing)))
    blocked = jnp.transpose(blocked, axis_order)
    return blocked.reshape((level_count, row_count, col_count) + trailing)


def window_pass(inputs, cotangent, labels, in_weight, out_weight, bias_full):
    highest = lax.Precision.HIGH
    average = jnp.mean(inputs, axis=-1, keepdims=True)
    centered = inputs - average
    variance = jnp.mean(centered * centered, axis=-1, keepdims=True)
    inv_std = lax.rsqrt(variance + 1e-05)
    normed = centered * inv_std
    projected = jnp.einsum("wtc,cf->wtf", normed, in_weight, precision=highest)
    win_count, tok_count = (inputs.shape[0], inputs.shape[1])
    heads_split = projected.reshape(win_count, tok_count, 3, HEADS, HEAD_DIM)
    queries = heads_split[:, :, 0]
    key_vecs = heads_split[:, :, 1]
    value_vecs = heads_split[:, :, 2]
    factor = HEAD_DIM ** (-0.5)
    scores = (
        jnp.einsum("wqhd,wkhd->whqk", queries, key_vecs, precision=highest) * factor
        + bias_full[None]
    )
    allowed = (labels[:, :, None] == labels[:, None, :]) & (labels[:, None, :] > 0.5)
    scores = jnp.where(allowed[:, None], scores, -1000000000.0)
    peak = jnp.max(scores, axis=-1, keepdims=True)
    exponent = jnp.exp(scores - peak)
    probs = exponent / jnp.sum(exponent, axis=-1, keepdims=True)
    attended = jnp.einsum("whqk,wkhd->wqhd", probs, value_vecs, precision=highest).reshape(
        win_count, tok_count, WIDTH
    )
    grad_attended = jnp.einsum("wte,ce->wtc", cotangent, out_weight, precision=highest)
    grad_out_part = jnp.einsum(
        "wtc,wte->ce", attended, cotangent, precision=highest
    )
    grad_heads = grad_attended.reshape(win_count, tok_count, HEADS, HEAD_DIM)
    grad_probs = jnp.einsum("wqhd,wkhd->whqk", grad_heads, value_vecs, precision=highest)
    grad_values = jnp.einsum("whqk,wqhd->wkhd", probs, grad_heads, precision=highest)
    grad_scores = probs * (grad_probs - jnp.sum(grad_probs * probs, axis=-1, keepdims=True))
    grad_queries = jnp.einsum("whqk,wkhd->wqhd", grad_scores, key_vecs, precision=highest) * factor
    grad_keys = jnp.einsum("whqk,wqhd->wkhd", grad_scores, queries, precision=highest) * factor
    score_sum = jnp.sum(grad_scores, axis=0)
    grad_values = grad_values.reshape(win_count, tok_count, WIDTH)
    grad_in_values = jnp.einsum("wtc,wtf->cf", normed, grad_values, precision=highest)
    grad_pairs = jnp.stack([grad_queries, grad_keys], axis=2).reshape(
        win_count, tok_count, 2 * WIDTH
    )
    grad_in_pairs = jnp.einsum("wtc,wtf->cf", normed, grad_pairs, precision=highest)
    grad_projected = jnp.concatenate([grad_pairs, grad_values], axis=2)
    grad_normed = jnp.einsum("wtf,cf->wtc", grad_projected, in_weight, precision=highest)
    grad_inputs = inv_std * (
        grad_normed
        - jnp.mean(grad_normed, axis=-1, keepdims=True)
        - normed * jnp.mean(grad_normed * normed, axis=-1, keepdims=True)
    )
    return (grad_inputs, grad_in_pairs, grad_in_values, grad_out_part, score_sum)


def rounded(value):
    return lax.reduce_precision(value, exponent_bits=8, mantissa_bits=7)


def three_terms(value, axis):
    first = rounded(value)
    second = rounded(value - first)
    third = rounded(value - first - second)
    return jnp.concatenate([first, second, third], axis=axis).astype(jnp.bfloat16)


def body(fields, grad_out, region_ids, bias_index, bias_table, in_weight, out_weight):
    level_count, row_count, col_count, width = fields.shape
    half_rows = WIN_LAT // 2
    half_cols = WIN_LON // 2
    token_count = bias_index.shape[0]
    table_rows, head_count = bias_table.shape
    lon_count = lax.axis_size("lon")
    lat_count = lax.axis_size("lat")
    device_count = lon_count * lat_count
    device = lax.axis_index("lon") * lat_count + lax.axis_index("lat")
    pair_count = token_count * token_count // device_count
    own_index = lax.dynamic_slice_in_dim(
        bias_index.reshape(-1), device * pair_count, pair_count, 0
    )
    one_hot = (
        own_index[:, None] == jnp.arange(table_rows, dtype=jnp.int32)[None, :]
    ).astype(jnp.bfloat16)
    found = lax.dot_general(
        three_terms(bias_table, 1), one_hot, (((0,), (1,)), ((), ())),
        preferred_element_type=jnp.float32,
    )
    found = found[:head_count] + found[head_count : 2 * head_count] + found[2 * head_count :]
    labels = (region_ids + 1).astype(jnp.float32)
    label_lanes = jnp.broadcast_to(labels[..., None], labels.shape + (128,))
    block = jnp.concatenate([fields, grad_out, label_lanes], axis=3)
    block = jnp.concatenate(
        [block[:, :, half_cols:], shifted(block[:, :, :half_cols], "lon", -1)], axis=2
    )
    block = jnp.concatenate(
        [shifted(block[:, row_count - half_rows :], "lat", 1), block[:, : row_count - half_rows]],
        axis=1,
    )
    block, found = lax.optimization_barrier((block, found))
    gathered = doubled(doubled(found[None], "lat")[None], "lon").reshape(
        device_count, head_count, pair_count
    )
    bias_full = jnp.transpose(gathered, (1, 0, 2)).reshape(head_count, token_count, token_count)

    frame_in = block[..., :width]
    frame_grad = block[..., width : 2 * width]
    wrapped = (lax.axis_index("lat") == 0) & (jnp.arange(row_count) < half_rows)
    frame_labels = block[..., 2 * width] + jnp.where(wrapped, 3.0, 0.0)[None, :, None]
    grad_win, grad_in_pairs, grad_in_values, grad_out_part, score_sum = window_pass(
        split_windows(frame_in),
        split_windows(frame_grad),
        split_windows(frame_labels),
        in_weight,
        out_weight,
        bias_full,
    )
    own_rows = width // lon_count
    split = (lon_count, lat_count, own_rows // lat_count, 2 * width)
    lon_bits = [("lon", bit) for bit in range(bit_count("lon"))]
    lat_bits = [("lat", bit) for bit in range(bit_count("lat"))]
    late_part = jnp.concatenate([grad_in_values, grad_out_part], axis=1).reshape(split)
    late_steps = list(
        halved_steps(late_part, lon_bits[:1] + lat_bits[:1] + lon_bits[1:] + lat_bits[1:])
    )
    score_parts = jnp.transpose(
        score_sum.reshape(head_count, device_count, pair_count), (1, 0, 2)
    ).reshape(lon_count, lat_count, head_count, pair_count)
    score_chain = halved_steps(score_parts, lon_bits + lat_bits)
    first_sum = next(score_chain)
    own_scores = list(score_chain)[-1]
    grad_in_pairs, _ = lax.optimization_barrier((grad_in_pairs, first_sum))
    pair_steps = list(halved_steps(grad_in_pairs.reshape(split), lon_bits + lat_bits))
    late_weights = doubled(late_steps[-1][None], "lat").reshape(own_rows, 2 * width)
    pair_weights = doubled(pair_steps[-1][None], "lat").reshape(own_rows, 2 * width)
    found = jnp.dot(three_terms(own_scores, 0), one_hot, preferred_element_type=jnp.float32)
    found = found[:head_count] + found[head_count : 2 * head_count] + found[2 * head_count :]
    found = jnp.transpose(
        found.reshape(head_count, lon_count, table_rows // lon_count), (1, 0, 2)
    )
    grad_bias = jnp.transpose(swapped_sum(halved_sum(found, "lon")[0], "lat"))
    grad_frame = join_windows(grad_win, level_count, row_count, col_count)
    grad_frame = jnp.concatenate(
        [grad_frame[:, half_rows:], shifted(grad_frame[:, :half_rows], "lat", -1)], axis=1
    )
    grad_frame = jnp.concatenate(
        [
            shifted(grad_frame[:, :, col_count - half_cols :], "lon", 1),
            grad_frame[:, :, : col_count - half_cols],
        ],
        axis=2,
    )
    grad_in_weight = jnp.concatenate([pair_weights, late_weights[:, :width]], axis=1)
    return (grad_out + grad_frame, grad_in_weight, late_weights[:, width:], grad_bias)


def solution(mesh):
    in_specs = (
        P(None, "lat", "lon", None),
        P(None, "lat", "lon", None),
        P(None, "lat", "lon"),
        P(),
        P(),
        P(),
        P(),
    )
    out_specs = (P(None, "lat", "lon", None), P("lon", None), P("lon", None), P("lon", None))
    return jax.shard_map(body, mesh=mesh, in_specs=in_specs, out_specs=out_specs, check_vma=False)
```

```python
import jax
import jax.numpy as jnp
from jax import lax
from jax.sharding import PartitionSpec as P

WIDTH = 512
HEADS = 16
HEAD_DIM = 32
WIN_LAT = 12
WIN_LON = 6


def shifted(value, axis, steps):
    count = lax.axis_size(axis)
    pairs = [(source, (source + steps) % count) for source in range(count)]
    return lax.ppermute(value, axis, pairs)


def bit_count(axis):
    count = lax.axis_size(axis)
    assert count & (count - 1) == 0
    return count.bit_length() - 1


def swapped(value, axis, bit):
    count = lax.axis_size(axis)
    return lax.ppermute(value, axis, [(i, i ^ (1 << bit)) for i in range(count)])


def halved_sum(value, axis):
    index = lax.axis_index(axis)
    for bit in range(bit_count(axis)):
        value = value.reshape((value.shape[0] // 2, 2) + value.shape[1:])
        side = (index >> bit) & 1
        kept = lax.dynamic_index_in_dim(value, side, 1, keepdims=False)
        given = lax.dynamic_index_in_dim(value, 1 - side, 1, keepdims=False)
        value = kept + swapped(given, axis, bit)
    return value


def halved_together(values, orders):
    bits = [(axis, bit) for axis in ("lon", "lat") for bit in reversed(range(bit_count(axis)))]
    values = [value.reshape((2,) * len(bits) + value.shape[2:]) for value in values]
    left = [list(bits) for _ in values]
    for steps in zip(*orders):
        for item, (axis, bit) in enumerate(steps):
            dim = left[item].index((axis, bit))
            left[item].remove((axis, bit))
            side = (lax.axis_index(axis) >> bit) & 1
            kept = lax.dynamic_index_in_dim(values[item], side, dim, keepdims=False)
            given = lax.dynamic_index_in_dim(values[item], 1 - side, dim, keepdims=False)
            values[item] = kept + swapped(given, axis, bit)
        values = list(lax.optimization_barrier(tuple(values)))
    return values


def doubled(value, axis):
    index = lax.axis_index(axis)
    for bit in reversed(range(bit_count(axis))):
        other = swapped(value, axis, bit)
        upper = ((index >> bit) & 1) == 1
        low = jnp.where(upper, other, value)
        high = jnp.where(upper, value, other)
        value = jnp.stack([low, high], axis=1)
        value = value.reshape((value.shape[0] * 2,) + value.shape[2:])
    return value


def swapped_sum(value, axis):
    for bit in range(bit_count(axis)):
        value = value + swapped(value, axis, bit)
    return value


def split_windows(array):
    level_count, row_count, col_count = array.shape[:3]
    trailing = array.shape[3:]
    blocked = array.reshape(
        (level_count, row_count // WIN_LAT, WIN_LAT, col_count // WIN_LON, WIN_LON) + trailing
    )
    axis_order = (1, 3, 0, 2, 4) + tuple(range(5, 5 + len(trailing)))
    blocked = jnp.transpose(blocked, axis_order)
    return blocked.reshape(
        (row_count // WIN_LAT * (col_count // WIN_LON), level_count * WIN_LAT * WIN_LON) + trailing
    )


def join_windows(windows, level_count, row_count, col_count):
    trailing = windows.shape[2:]
    blocked = windows.reshape(
        (row_count // WIN_LAT, col_count // WIN_LON, level_count, WIN_LAT, WIN_LON) + trailing
    )
    axis_order = (2, 0, 3, 1, 4) + tuple(range(5, 5 + len(trailing)))
    blocked = jnp.transpose(blocked, axis_order)
    return blocked.reshape((level_count, row_count, col_count) + trailing)


def window_pass(inputs, cotangent, labels, in_weight, out_weight, bias_full):
    highest = lax.Precision.HIGH
    average = jnp.mean(inputs, axis=-1, keepdims=True)
    centered = inputs - average
    variance = jnp.mean(centered * centered, axis=-1, keepdims=True)
    inv_std = lax.rsqrt(variance + 1e-05)
    normed = centered * inv_std
    projected = jnp.einsum("wtc,cf->wtf", normed, in_weight, precision=highest)
    win_count, tok_count = (inputs.shape[0], inputs.shape[1])
    heads_split = projected.reshape(win_count, tok_count, 3, HEADS, HEAD_DIM)
    queries = heads_split[:, :, 0]
    key_vecs = heads_split[:, :, 1]
    value_vecs = heads_split[:, :, 2]
    factor = HEAD_DIM ** (-0.5)
    scores = (
        jnp.einsum("wqhd,wkhd->whqk", queries, key_vecs, precision=highest) * factor
        + bias_full[None]
    )
    allowed = (labels[:, :, None] == labels[:, None, :]) & (labels[:, None, :] > 0.5)
    scores = jnp.where(allowed[:, None], scores, -1000000000.0)
    peak = jnp.max(scores, axis=-1, keepdims=True)
    exponent = jnp.exp(scores - peak)
    probs = exponent / jnp.sum(exponent, axis=-1, keepdims=True)
    attended = jnp.einsum("whqk,wkhd->wqhd", probs, value_vecs, precision=highest).reshape(
        win_count, tok_count, WIDTH
    )
    grad_attended = jnp.einsum("wte,ce->wtc", cotangent, out_weight, precision=highest)
    grad_out_part = jnp.einsum(
        "wtc,wte->ce", attended, cotangent, precision=highest
    )
    grad_heads = grad_attended.reshape(win_count, tok_count, HEADS, HEAD_DIM)
    grad_probs = jnp.einsum("wqhd,wkhd->whqk", grad_heads, value_vecs, precision=highest)
    grad_values = jnp.einsum("whqk,wqhd->wkhd", probs, grad_heads, precision=highest)
    grad_scores = probs * (grad_probs - jnp.sum(grad_probs * probs, axis=-1, keepdims=True))
    grad_queries = jnp.einsum("whqk,wkhd->wqhd", grad_scores, key_vecs, precision=highest) * factor
    grad_keys = jnp.einsum("whqk,wqhd->wkhd", grad_scores, queries, precision=highest) * factor
    score_sum = jnp.sum(grad_scores, axis=0)
    grad_values = grad_values.reshape(win_count, tok_count, WIDTH)
    grad_in_values = jnp.einsum("wtc,wtf->cf", normed, grad_values, precision=highest)
    grad_pairs = jnp.stack([grad_queries, grad_keys], axis=2).reshape(
        win_count, tok_count, 2 * WIDTH
    )
    grad_in_pairs = jnp.einsum("wtc,wtf->cf", normed, grad_pairs, precision=highest)
    grad_projected = jnp.concatenate([grad_pairs, grad_values], axis=2)
    grad_normed = jnp.einsum("wtf,cf->wtc", grad_projected, in_weight, precision=highest)
    grad_inputs = inv_std * (
        grad_normed
        - jnp.mean(grad_normed, axis=-1, keepdims=True)
        - normed * jnp.mean(grad_normed * normed, axis=-1, keepdims=True)
    )
    return (grad_inputs, grad_in_pairs, grad_in_values, grad_out_part, score_sum)


def rounded(value):
    return lax.reduce_precision(value, exponent_bits=8, mantissa_bits=7)


def three_terms(value, axis):
    first = rounded(value)
    second = rounded(value - first)
    third = rounded(value - first - second)
    return jnp.concatenate([first, second, third], axis=axis).astype(jnp.bfloat16)


def body(fields, grad_out, region_ids, bias_index, bias_table, in_weight, out_weight):
    level_count, row_count, col_count, width = fields.shape
    half_rows = WIN_LAT // 2
    half_cols = WIN_LON // 2
    token_count = bias_index.shape[0]
    table_rows, head_count = bias_table.shape
    lon_count = lax.axis_size("lon")
    lat_count = lax.axis_size("lat")
    device_count = lon_count * lat_count
    device = lax.axis_index("lon") * lat_count + lax.axis_index("lat")
    pair_count = token_count * token_count // device_count
    own_index = lax.dynamic_slice_in_dim(
        bias_index.reshape(-1), device * pair_count, pair_count, 0
    )
    one_hot = (
        own_index[:, None] == jnp.arange(table_rows, dtype=jnp.int32)[None, :]
    ).astype(jnp.bfloat16)
    found = lax.dot_general(
        three_terms(bias_table, 1), one_hot, (((0,), (1,)), ((), ())),
        preferred_element_type=jnp.float32,
    )
    found = found[:head_count] + found[head_count : 2 * head_count] + found[2 * head_count :]
    labels = (region_ids + 1).astype(jnp.float32)
    label_lanes = jnp.broadcast_to(labels[..., None], labels.shape + (128,))
    block = jnp.concatenate([fields, grad_out, label_lanes], axis=3)
    block = jnp.concatenate(
        [block[:, :, half_cols:], shifted(block[:, :, :half_cols], "lon", -1)], axis=2
    )
    block = jnp.concatenate(
        [shifted(block[:, row_count - half_rows :], "lat", 1), block[:, : row_count - half_rows]],
        axis=1,
    )
    block, found = lax.optimization_barrier((block, found))
    gathered = doubled(doubled(found[None], "lat")[None], "lon").reshape(
        device_count, head_count, pair_count
    )
    bias_full = jnp.transpose(gathered, (1, 0, 2)).reshape(head_count, token_count, token_count)

    frame_in = block[..., :width]
    frame_grad = block[..., width : 2 * width]
    wrapped = (lax.axis_index("lat") == 0) & (jnp.arange(row_count) < half_rows)
    frame_labels = block[..., 2 * width] + jnp.where(wrapped, 3.0, 0.0)[None, :, None]
    grad_win, grad_in_pairs, grad_in_values, grad_out_part, score_sum = window_pass(
        split_windows(frame_in),
        split_windows(frame_grad),
        split_windows(frame_labels),
        in_weight,
        out_weight,
        bias_full,
    )
    own_rows = width // lon_count
    split = (lon_count, lat_count, own_rows // lat_count, 2 * width)
    lon_bits = [("lon", bit) for bit in range(bit_count("lon"))]
    lat_bits = [("lat", bit) for bit in range(bit_count("lat"))]
    late_part = jnp.concatenate([grad_in_values, grad_out_part], axis=1).reshape(split)
    score_parts = jnp.transpose(
        score_sum.reshape(head_count, device_count, pair_count), (1, 0, 2)
    ).reshape(lon_count, lat_count, head_count, pair_count)
    own_scores, late_sum, pair_sum = halved_together(
        [score_parts, late_part, grad_in_pairs.reshape(split)],
        [
            lon_bits + lat_bits,
            lon_bits[:1] + lat_bits[:1] + lon_bits[1:] + lat_bits[1:],
            lon_bits + lat_bits,
        ],
    )
    late_weights = doubled(late_sum[None], "lat").reshape(own_rows, 2 * width)
    pair_weights = doubled(pair_sum[None], "lat").reshape(own_rows, 2 * width)
    found = jnp.dot(three_terms(own_scores, 0), one_hot, preferred_element_type=jnp.float32)
    found = found[:head_count] + found[head_count : 2 * head_count] + found[2 * head_count :]
    found = jnp.transpose(
        found.reshape(head_count, lon_count, table_rows // lon_count), (1, 0, 2)
    )
    grad_bias = jnp.transpose(swapped_sum(halved_sum(found, "lon")[0], "lat"))
    grad_frame = join_windows(grad_win, level_count, row_count, col_count)
    grad_frame = jnp.concatenate(
        [grad_frame[:, half_rows:], shifted(grad_frame[:, :half_rows], "lat", -1)], axis=1
    )
    grad_frame = jnp.concatenate(
        [
            shifted(grad_frame[:, :, col_count - half_cols :], "lon", 1),
            grad_frame[:, :, : col_count - half_cols],
        ],
        axis=2,
    )
    grad_in_weight = jnp.concatenate([pair_weights, late_weights[:, :width]], axis=1)
    return (grad_out + grad_frame, grad_in_weight, late_weights[:, width:], grad_bias)


def solution(mesh):
    in_specs = (
        P(None, "lat", "lon", None),
        P(None, "lat", "lon", None),
        P(None, "lat", "lon"),
        P(),
        P(),
        P(),
        P(),
    )
    out_specs = (P(None, "lat", "lon", None), P("lon", None), P("lon", None), P("lon", None))
    return jax.shard_map(body, mesh=mesh, in_specs=in_specs, out_specs=out_specs, check_vma=False)
```
